32 devices in a mesh: groups: 2 (over x), ctx: 4 (over y, core), head: 4 (over z).
Axes of the slice: x: 2, y: 2, z: 4, core: 2. Of those that a mesh axis runs over, the one named last changes fastest.
Arguments:
- xs: bfloat16 [12288, 4096], P(('groups', 'ctx', 'head')), parts along dimension 0, may hold values from -6 to 6
- gate_in: bfloat16 [12288, 4096], P(('groups', 'ctx', 'head')), parts along dimension 0, may hold values from -6 to 6
- bc: bfloat16 [12288, 256], P(('groups', 'ctx', 'head')), parts along dimension 0, may hold values from -1.78125 to 1.78125
- dt_raw: bfloat16 [12288, 64], P(('groups', 'ctx', 'head')), parts along dimension 0, may hold values from -4 to 4
- doc_ids: int32 [12288], P(('groups', 'ctx')), parts along dimension 0, may hold values from 0 to 31, never falling along the last dimension, each value on 1 to 3072 neighbouring positions
- dt_bias: float32 [64], P('head'), may hold values from -1 to 1
- decay_rate: float32 [64], P('head'), may hold values from 8.138021e-06 to 0.03
- skip: float32 [64], P('head'), may hold values from 0.5 to 1.5
- norm_gain: float32 [4096], replicated, may hold values from 0.5 to 1.5
Outputs:
- mixed: bfloat16 [12288, 4096], P(('groups', 'ctx', 'head')), parts along dimension 0
The draws below stay inside these ranges and needn't reach their ends.
There are 2 independent parts, one for each index of `groups`. The reference program is written for one: setup_inputs(seed, part) draws one part's arguments, and reference() takes and returns one part's arrays. A program takes and returns all parts, laid end to end along the dimension named above; an argument that names none is the same for every part. Nothing has to cross between parts.
Inputs may be any that keep to these rules, and one draw needn't show every extreme that they name: `doc_ids`: document ids never fall along the window; each document is one run of tokens, at most 3072 long, and one document is exactly that long.
All inputs are finite; a program needn't handle non-finite values.
Results may differ from the reference program's by a relative error of at most 0.007.
Values may be sent and summed in bfloat16 or wider, within the bound.
A program may use at most 64 MiB of HBM per device.

```python
import math
import jax
import jax.numpy as jnp
import numpy as np
from jax import lax

HEADS = 64
HDIM = 64
STATE = 128
STRETCH = 256
DOCS = 32
TOKENS = 6144


def block_levels(own_key, extent, shards, low, high):
    factor_of = 1.0
    for axis_at, shards_of in shards:
        steps = jax.random.uniform(jax.random.fold_in(jax.random.fold_in(own_key, 6), axis_at), (shards_of,), jnp.float32, low / len(shards), high / len(shards))
        factor_of = factor_of * jnp.repeat(jnp.exp(steps), extent[axis_at] // shards_of).reshape((-1,) + (1,) * (len(extent) - 1 - axis_at))
    return factor_of


def split_up(number_of, total, bound, lean):
    loads = [(1 << 20) // math.isqrt(standing ** lean) + 1 for standing in range(2, number_of + 1)]
    surplus, holding = total - bound - (number_of - 1), [1] * (number_of - 1)
    while surplus > 0:
        free = [i for i in range(number_of - 1) if holding[i] < bound]
        pool, budget = sum([loads[i] for i in free]), surplus
        for i in free:
            more = min(bound - holding[i], max(1, budget * loads[i] // pool), surplus)
            holding[i] = holding[i] + more
            surplus = surplus - more
    return np.array([bound] + holding)


def uneven(key, count, total, most, skew):
    if count == 2:
        one = jax.random.randint(key, (), max(1, total - most), min(most, total - 1) + 1)
        return jnp.stack([one, total - one])
    sizes = jnp.asarray(split_up(count, total, most, skew), jnp.int32)
    twos = (count - 1) // 2
    donor, receiver = sizes[1:1 + 2 * twos:2], sizes[2:2 + 2 * twos:2]
    room = jnp.minimum(donor - 1, most - receiver)
    moved = jax.random.randint(jax.random.fold_in(key, 1), (twos,), 0, 1 << 20) % (room + 1)
    sizes = sizes.at[1:1 + 2 * twos:2].set(donor - moved).at[2:2 + 2 * twos:2].set(receiver + moved)
    return sizes[jax.random.permutation(jax.random.fold_in(key, 2), count)]


def bell_draw(stream_key, shape, scale, reach, cuts=(), dtype=jnp.bfloat16):
    values = scale * jax.random.normal(stream_key, shape, jnp.float32)
    if cuts:
        values = values * block_levels(stream_key, shape, cuts, -0.22, 0.18)
    return jnp.clip(values, -reach, reach).astype(dtype)


def setup_inputs(seed: int = 0, part: int = 0) -> dict:
    splits = jax.random.split(jax.random.key(seed), 10)
    part_keys = jax.random.split(jax.random.fold_in(splits[9], part), 10)
    return {
        "xs": bell_draw(part_keys[0], (TOKENS, HEADS * HDIM), 1.0, 6.0, ((0, 16),)),
        "gate_in": bell_draw(part_keys[1], (TOKENS, HEADS * HDIM), 1.0, 6.0, ((0, 16),)),
        "bc": bell_draw(part_keys[2], (TOKENS, 2 * STATE), (STATE ** -0.25), 1.78125, ((0, 16),)),
        "dt_raw": bell_draw(part_keys[3], (TOKENS, HEADS), 1.0, 4.0, ((0, 16),)),
        "doc_ids": jnp.searchsorted(jnp.cumsum(uneven(part_keys[4], DOCS, TOKENS, TOKENS // 2, 2)), jnp.arange(TOKENS), side="right").astype(jnp.int32),
        "dt_bias": jnp.clip(jax.random.uniform(splits[5], (HEADS,), jnp.float32, -1.0, 1.0) * block_levels(splits[5], (HEADS,), ((0, 4),), -0.4, 0.0), -1.0, 1.0),
        "decay_rate": jnp.clip(jnp.exp(math.log(0.03) - 8.2124056 * jax.random.uniform(splits[6], (HEADS,), jnp.float32) ** block_levels(splits[6], (HEADS,), ((0, 4),), -0.2, 0.2)), 8.138021257764194e-06, 0.03),
        "skip": jnp.clip(0.5 + 1.0 * jax.random.uniform(splits[7], (HEADS,), jnp.float32) ** block_levels(splits[7], (HEADS,), ((0, 4),), -0.2, 0.2), 0.5, 1.5),
        "norm_gain": jnp.clip(1.0 + 0.1 * jax.random.normal(splits[8], (HEADS * HDIM,), jnp.float32), 0.5, 1.5),
    }


def apply_state(c_rows, state):
    state_hi = state.astype(jnp.bfloat16)
    state_lo = (state - state_hi.astype(jnp.float32)).astype(jnp.bfloat16)
    first = jnp.einsum('tn,hpn->thp', c_rows.astype(jnp.float32), state_hi.astype(jnp.float32))
    second = jnp.einsum('tn,hpn->thp', c_rows.astype(jnp.float32), state_lo.astype(jnp.float32))
    return first + second

def block_step(entering, pieces):
    head_x, in_b, in_c, dt_block, log_block, ids_block, before = pieces
    scores = jnp.dot(in_c, in_b.T, preferred_element_type=jnp.float32)
    lower = jnp.arange(STRETCH)[:, None] >= jnp.arange(STRETCH)[None, :]
    allowed = lower & (ids_block[:, None] == ids_block[None, :])
    spread = log_block[:, None, :] - log_block[None, :, :]
    decayed = jnp.exp(jnp.where(allowed[:, :, None], spread, -jnp.inf))
    mixing = (scores[:, :, None] * decayed * dt_block[None, :, :]).astype(jnp.bfloat16)
    x_float = head_x.astype(jnp.float32)
    local_y = jnp.einsum('tsh,shp->thp', mixing.astype(jnp.float32), x_float)
    last_id = ids_block[-1]
    log_end = log_block[-1]
    factor = jnp.where((ids_block == last_id)[:, None], jnp.exp(log_end[None, :] - log_block) * dt_block, 0.0)
    weighted = (factor[:, :, None] * x_float).astype(jnp.bfloat16)
    block_state = jnp.einsum('shp,sn->hpn', weighted.astype(jnp.float32), in_b.astype(jnp.float32))
    inside = ids_block == before
    applied = apply_state(in_c, entering)
    carried_y = jnp.where(inside[:, None, None], jnp.exp(log_block)[:, :, None] * applied, 0.0)
    keep = jnp.where(last_id == before, 1.0, 0.0).astype(jnp.float32)
    leaving = (keep * jnp.exp(log_end))[:, None, None] * entering + block_state
    return (leaving, (local_y, carried_y))

def reference(xs, gate_in, bc, dt_raw, doc_ids, dt_bias, decay_rate, skip, norm_gain):
    blocks = TOKENS // STRETCH
    head_x = xs.reshape(blocks, STRETCH, HEADS, HDIM)
    in_b = bc[:, :STATE].reshape(blocks, STRETCH, STATE)
    in_c = bc[:, STATE:].reshape(blocks, STRETCH, STATE)
    step_size = jax.nn.softplus(dt_raw.astype(jnp.float32) + dt_bias[None, :]).reshape(blocks, STRETCH, HEADS)
    log_decay = jnp.cumsum(-decay_rate[None, None, :] * step_size, axis=1)
    ids = doc_ids.reshape(blocks, STRETCH).astype(jnp.int32)
    before = jnp.concatenate([jnp.full((1,), -1, jnp.int32), ids[:-1, -1]])
    start = jnp.zeros((HEADS, HDIM, STATE), jnp.float32)
    unused, parts = lax.scan(block_step, start, (head_x, in_b, in_c, step_size, log_decay, ids, before))
    local_y, carried_y = parts
    ssm_out = local_y + carried_y + skip[None, None, :, None] * head_x.astype(jnp.float32)
    ssm_out = ssm_out.astype(jnp.bfloat16).reshape(TOKENS, HEADS * HDIM)
    gated = ssm_out.astype(jnp.float32) * jax.nn.silu(gate_in.astype(jnp.float32))
    scale = lax.rsqrt(lax.optimization_barrier(jnp.mean(gated * gated, axis=-1, keepdims=True)) + 1e-05)
    return (gated * scale * norm_gain[None, :]).astype(jnp.bfloat16)
```

```python
import jax
import jax.numpy as jnp
from jax import lax
from jax.sharding import PartitionSpec as P

STATE = 128
EXTRA = 16
SPAN_AXES = ("ctx", "head")


def shards(xs, gate_in, bc, dt_raw, doc_ids, dt_bias, decay_rate, skip, norm_gain):
    f32, bf16 = jnp.float32, jnp.bfloat16
    tokens, columns = xs.shape
    heads = dt_raw.shape[1]
    hdim = columns // heads
    devices = lax.axis_size("ctx") * lax.axis_size("head")
    own = columns // devices
    params = lax.all_gather(
        jnp.stack([dt_bias, decay_rate, skip]), "head", axis=1, tiled=True
    )
    ids = lax.dynamic_slice(doc_ids, (lax.axis_index("head") * tokens,), (tokens,))
    dt = jax.nn.softplus(dt_raw.astype(f32) + params[0][None, :])
    lower = jnp.arange(tokens)[:, None] >= jnp.arange(tokens)[None, :]
    log_decay = -jnp.dot(
        lower.astype(f32), dt * params[1][None, :], precision=lax.Precision.HIGHEST
    )
    log_end = log_decay[-1]
    middle = 0.5 * log_end
    spread = lambda v: jnp.repeat(v, hdim, axis=-1)
    into = jnp.exp(middle[None, :] - log_decay) * dt
    out_of = jnp.exp(log_decay - middle[None, :])
    x = xs.astype(f32)
    weighted = (spread(into) * x).astype(bf16)
    in_b, in_c = bc[:, :STATE], bc[:, STATE:]
    scores = jnp.einsum("tn,sn->ts", in_c, in_b, preferred_element_type=f32)
    scores = jnp.where(lower & (ids[:, None] == ids[None, :]), scores, 0.0).astype(bf16)
    last_b = jnp.where((ids == ids[-1])[:, None], in_b, jnp.zeros_like(in_b))
    state = jnp.einsum("sn,sq->nq", last_b, weighted, preferred_element_type=f32)
    state = (state * spread(jnp.exp(middle))[None, :]).astype(bf16)
    factor = spread(jnp.exp(log_end))
    factor_hi = factor.astype(bf16)
    factor_lo = (factor - factor_hi.astype(f32)).astype(bf16)
    back = jnp.full((columns,), ids[-1].astype(bf16))
    extra = jnp.concatenate(
        [jnp.stack([factor_hi, factor_lo, back]), jnp.zeros((EXTRA - 3, columns), bf16)]
    )
    block = jnp.concatenate([state, extra])
    block = block.reshape(STATE + EXTRA, devices, own).transpose(1, 0, 2)
    got = lax.all_to_all(block, SPAN_AXES, split_axis=0, concat_axis=0, tiled=True)

    def advance(carry, piece):
        entering, before = carry
        mult = piece[STATE].astype(f32) + piece[STATE + 1].astype(f32)
        back_id = piece[STATE + 2].astype(f32)
        give = jnp.concatenate(
            [
                entering.astype(bf16),
                before[None].astype(bf16),
                jnp.zeros((EXTRA - 1, own), bf16),
            ]
        )
        keep = jnp.where(back_id == before, mult, 0.0)
        return (keep[None] * entering + piece[:STATE].astype(f32), back_id), give

    unused, give = lax.scan(
        advance, (jnp.zeros((STATE, own), f32), jnp.full((own,), -1.0, f32)), got
    )
    back_here = lax.all_to_all(give, SPAN_AXES, split_axis=0, concat_axis=0, tiled=True)
    back_here = back_here.transpose(1, 0, 2).reshape(STATE + EXTRA, columns)
    before = back_here[STATE, 0].astype(f32)
    inside_c = jnp.where((ids.astype(f32) == before)[:, None], in_c, jnp.zeros_like(in_c))
    carried = jnp.dot(inside_c, back_here[:STATE], preferred_element_type=f32)
    local = jnp.dot(scores, weighted, preferred_element_type=f32)
    ssm = (
        spread(out_of) * (local + carried * spread(jnp.exp(middle))[None, :])
        + spread(params[2])[None, :] * x
    )
    gated = ssm.astype(bf16).astype(f32) * jax.nn.silu(gate_in.astype(f32))
    scale = lax.rsqrt(jnp.mean(gated * gated, axis=-1, keepdims=True) + 1e-05)
    return (gated * scale * norm_gain[None, :]).astype(bf16)


def solution(mesh):
    rows = P(("groups", "ctx", "head"), None)
    return jax.shard_map(
        shards,
        mesh=mesh,
        in_specs=(rows, rows, rows, rows, P(("groups", "ctx")), P("head"), P("head"), P("head"), P()),
        out_specs=rows,
        check_vma=False,
    )
```

```python
import functools

import jax
import jax.numpy as jnp
from jax import lax
from jax.experimental import pallas as pl
from jax.experimental.pallas import tpu as pltpu
from jax.sharding import PartitionSpec as P

STATE = 128
EXTRA = 16
ROWS = STATE + EXTRA
MESH = pl.DeviceIdType.MESH
f32, bf16 = jnp.float32, jnp.bfloat16


def two_parts(v):
    hi = v.astype(bf16)
    return hi, (v - hi.astype(f32)).astype(bf16)


def dot(a, b):
    return jnp.dot(a, b, preferred_element_type=f32)


def kernel(
    n_ctx, n_head, owners,
    x_hbm, gate_hbm, bc, dt_raw, ids_col, ids_row, mine, gain,
    out_ref,
    x, gate, weighted, local, silu, square, into_s, out_s, decay_s, scores_s, last_b, rows_s, par,
    send1, recv1, send2, recv2,
    load_sem, par_ssem, par_rsem, ssem1, rsem1, ssem2, rsem2,
):
    tokens, columns = x.shape
    heads = dt_raw.shape[1]
    hdim = columns // heads
    own = columns // owners
    devices = n_ctx * n_head
    my_ctx, my_head = lax.axis_index("ctx"), lax.axis_index("head")
    me = my_ctx * n_head + my_head

    def place(d):
        return {"ctx": d // n_head, "head": lax.rem(d, n_head)}

    load_x = pltpu.make_async_copy(x_hbm, x, load_sem.at[0])
    load_gate = pltpu.make_async_copy(gate_hbm, gate, load_sem.at[1])
    load_x.start()
    load_gate.start()

    barrier = pltpu.get_barrier_semaphore()

    def greet(k, carry):
        peer = lax.rem(me + k, devices)
        pl.semaphore_signal(barrier, inc=1, device_id=place(peer), device_id_type=MESH)
        return carry

    lax.fori_loop(1, devices, greet, 0)
    pl.semaphore_wait(barrier, devices - 1)

    def par_copy(slot, peer, sem):
        return pltpu.make_async_remote_copy(
            src_ref=mine, dst_ref=par.at[slot],
            send_sem=par_ssem.at[sem], recv_sem=par_rsem.at[slot],
            device_id={"head": peer}, device_id_type=MESH,
        )

    for k in range(1, n_head):
        peer = lax.rem(my_head + k, n_head)
        par_copy(my_head, peer, peer).start()

    in_b, in_c = bc[:, :STATE], bc[:, STATE:]
    scores = lax.dot_general(in_c, in_b, (((1,), (1,)), ((), ())), preferred_element_type=f32)
    lower = lax.broadcasted_iota(jnp.int32, (tokens, tokens), 0) >= lax.broadcasted_iota(
        jnp.int32, (tokens, tokens), 1
    )
    same = ids_col[...] == ids_row[...]
    scores_s[...] = jnp.where(lower & same, scores, 0.0).astype(bf16)
    last_id = ids_row[:, tokens - 1 : tokens]
    last_b[...] = jnp.where(ids_col[...] == last_id, in_b.astype(f32), 0.0).astype(bf16)

    for k in range(1, n_head):
        peer = lax.rem(my_head + k, n_head)
        par_copy(peer, peer, peer).wait_recv()
    par[my_head] = mine[...]
    params = par[0]
    for k in range(1, n_head):
        params = params + par[k]
    bias, rate, skip = params[0:1, :heads], params[1:2, :heads], params[2:3, :heads]

    v = dt_raw[...].astype(f32) + bias
    dt = jnp.maximum(v, 0.0) + jnp.log1p(jnp.exp(-jnp.abs(v)))
    step = dt * rate
    step_hi, rest = two_parts(step)
    rest, step_lo = two_parts(step - step_hi.astype(f32))
    ones = lower.astype(f32).astype(bf16)
    log_decay = -(dot(ones, step_hi) + dot(ones, rest) + dot(ones, step_lo))
    log_end = log_decay[tokens - 1 : tokens, :]
    middle = 0.5 * log_end
    for ref, value in (
        (into_s, jnp.exp(middle - log_decay) * dt),
        (out_s, jnp.exp(log_decay - middle)),
        (decay_s, jnp.exp(log_decay)),
    ):
        ref[0], ref[1] = two_parts(value)
    at = lax.broadcasted_iota(jnp.int32, (EXTRA, heads), 0)
    end_row = jnp.exp(log_end)
    end_hi = end_row.astype(bf16).astype(f32)
    mid_row = jnp.exp(middle)
    mid_hi = mid_row.astype(bf16).astype(f32)
    skip_hi = skip.astype(bf16).astype(f32)
    pick = jnp.zeros((EXTRA, heads), f32)
    for i, row in enumerate(
        (end_hi, end_row - end_hi, last_id.astype(f32), mid_hi, mid_row - mid_hi, skip_hi, skip - skip_hi)
    ):
        pick = jnp.where(at == i, row, pick)
    rows_s[...] = pick.astype(bf16)
    load_x.wait()

    def selector(g):
        head = lax.broadcasted_iota(jnp.int32, (heads, own), 0)
        column = lax.broadcasted_iota(jnp.int32, (heads, own), 1) + g * own
        base = head * hdim
        return jnp.where((column >= base) & (column < base + hdim), 1.0, 0.0).astype(bf16)

    def spread(ref, sel):
        return dot(ref[0], sel) + dot(ref[1], sel)

    def part(g):
        return pl.ds(pl.multiple_of(g * own, own), own)

    def copy1(owner, slot, sem):
        return pltpu.make_async_remote_copy(
            src_ref=send1.at[owner], dst_ref=recv1.at[slot],
            send_sem=ssem1.at[owner], recv_sem=rsem1.at[sem],
            device_id=place(owner), device_id_type=MESH,
        )

    def copy2(peer, slot, sem):
        return pltpu.make_async_remote_copy(
            src_ref=send2.at[peer], dst_ref=recv2.at[slot],
            send_sem=ssem2.at[peer], recv_sem=rsem2.at[sem],
            device_id=place(peer), device_id_type=MESH,
        )

    def states(k, carry):
        g = lax.rem(me + k, owners)
        sel = selector(g)
        cols = part(g)
        w = (spread(into_s, sel) * x[:, cols].astype(f32)).astype(bf16)
        weighted[:, cols] = w
        extra = dot(rows_s[...], sel)
        mid = extra[3:4] + extra[4:5]
        state = lax.dot_general(
            last_b[...], w, (((0,), (0,)), ((), ())), preferred_element_type=f32
        )
        send1[g, 0:STATE, :] = (state * mid).astype(bf16)
        send1[g, STATE:ROWS, :] = extra.astype(bf16)

        @pl.when(g != me)
        def _():
            copy1(g, me, me).start()

        return carry

    lax.fori_loop(1, owners + 1, states, 0)
    load_gate.wait()

    def inside(g, carry):
        sel = selector(g)
        cols = part(g)
        extra = dot(rows_s[...], sel)
        skips = extra[5:6] + extra[6:7]
        y = dot(scores_s[...], weighted[:, cols])
        local[:, cols] = spread(out_s, sel) * y + skips * x[:, cols].astype(f32)
        v = gate[:, cols].astype(f32)
        silu[:, cols] = v / (1.0 + jnp.exp(-v))
        return carry

    lax.fori_loop(0, owners, inside, 0)

    def own_scan():
        recv1[me] = send1[me]

        def advance(j, carry):
            entering, before = carry

            @pl.when(j != me)
            def _():
                copy1(me, j, j).wait_recv()

            send2[j, 0:STATE, :] = entering.astype(bf16)
            send2[j, STATE:ROWS, :] = jnp.broadcast_to(before, (EXTRA, own)).astype(bf16)

            @pl.when(j != me)
            def _():
                copy2(j, me, me).start()

            tail = recv1[j, STATE:ROWS, :].astype(f32)
            back = tail[2:3]
            mult = jnp.where(back == before, tail[0:1] + tail[1:2], 0.0)
            entering = mult * entering + recv1[j, 0:STATE, :].astype(f32)
            return entering, back

        lax.fori_loop(
            0, devices, advance, (jnp.zeros((STATE, own), f32), jnp.full((1, own), -1.0, f32))
        )
        recv2[me] = send2[me]

    if owners == devices:
        own_scan()
    else:
        pl.when(me < owners)(own_scan)

    square[...] = jnp.zeros_like(square)

    def finish(k, carry):
        g = lax.rem(me + k, owners)

        @pl.when(g != me)
        def _():
            copy2(me, g, g).wait_recv()

        cols = part(g)
        before = recv2[g, STATE:ROWS, :].astype(f32)[0:1, 0:1]
        rows = jnp.where(ids_col[...].astype(f32) == before, in_c.astype(f32), 0.0).astype(bf16)
        carried = dot(rows, recv2[g, 0:STATE, :])
        ssm = local[:, cols] + spread(decay_s, selector(g)) * carried
        gated = ssm.astype(bf16).astype(f32) * silu[:, cols]
        local[:, cols] = gated
        total = square[...]
        for i in range(own // 128):
            piece = gated[:, i * 128 : (i + 1) * 128]
            total = total + piece * piece
        square[...] = total
        return carry

    lax.fori_loop(0, owners, finish, 0)
    mean = jnp.sum(square[...], axis=1, keepdims=True) * (1.0 / columns)
    scale = lax.rsqrt(mean + 1e-05)

    def store(g, carry):
        cols = part(g)
        out_ref[:, cols] = (local[:, cols] * scale * gain[:, cols]).astype(bf16)
        return carry

    lax.fori_loop(0, owners, store, 0)

    for k in range(1, n_head):
        peer = lax.rem(my_head + k, n_head)
        par_copy(my_head, peer, peer).wait_send()

    def drain1(g, carry):
        @pl.when(g != me)
        def _():
            copy1(g, me, me).wait_send()

        return carry

    lax.fori_loop(0, owners, drain1, 0)

    def drain2(j, carry):
        @pl.when(j != me)
        def _():
            copy2(j, me, me).wait_send()

        return carry

    def drain_all():
        lax.fori_loop(0, devices, drain2, 0)

    if owners == devices:
        drain_all()
    else:
        pl.when(me < owners)(drain_all)


def shards(xs, gate_in, bc, dt_raw, doc_ids, dt_bias, decay_rate, skip, norm_gain):
    tokens, columns = xs.shape
    heads = dt_raw.shape[1]
    n_ctx, n_head = lax.axis_size("ctx"), lax.axis_size("head")
    devices = n_ctx * n_head
    owners = min(devices, columns // 128)
    own = columns // owners
    at = lax.axis_index("head")
    ids = lax.dynamic_slice(doc_ids, (at * tokens,), (tokens,))
    stack = jnp.stack([dt_bias, decay_rate, skip])
    mine = jnp.where(
        (jnp.arange(heads) // (heads // n_head) == at)[None, :], jnp.tile(stack, (1, n_head)), 0.0
    )
    mine = jnp.pad(mine, ((0, 5), (0, 128 - heads)))
    vmem = pl.BlockSpec(memory_space=pltpu.VMEM)
    hbm = pl.BlockSpec(memory_space=pl.ANY)
    dma = pltpu.SemaphoreType.DMA
    return pl.pallas_call(
        functools.partial(kernel, n_ctx, n_head, owners),
        out_shape=jax.ShapeDtypeStruct((tokens, columns), bf16),
        in_specs=[hbm, hbm] + [vmem] * 6,
        out_specs=vmem,
        scratch_shapes=[
            pltpu.VMEM((tokens, columns), bf16),
            pltpu.VMEM((tokens, columns), bf16),
            pltpu.VMEM((tokens, columns), bf16),
            pltpu.VMEM((tokens, columns), f32),
            pltpu.VMEM((tokens, columns), f32),
            pltpu.VMEM((tokens, 128), f32),
            pltpu.VMEM((2, tokens, heads), bf16),
            pltpu.VMEM((2, tokens, heads), bf16),
            pltpu.VMEM((2, tokens, heads), bf16),
            pltpu.VMEM((tokens, tokens), bf16),
            pltpu.VMEM((tokens, STATE), bf16),
            pltpu.VMEM((EXTRA, heads), bf16),
            pltpu.VMEM((n_head, 8, 128), f32),
            pltpu.VMEM((owners, ROWS, own), bf16),
            pltpu.VMEM((devices, ROWS, own), bf16),
            pltpu.VMEM((devices, ROWS, own), bf16),
            pltpu.VMEM((owners, ROWS, own), bf16),
            dma((2,)), dma((n_head,)), dma((n_head,)),
            dma((owners,)), dma((devices,)), dma((devices,)), dma((owners,)),
        ],
        compiler_params=pltpu.CompilerParams(
            collective_id=0, has_side_effects=True, vmem_limit_bytes=52 * 2**20
        ),
        cost_estimate=pl.CostEstimate(
            flops=3 * 10**9, bytes_accessed=10**7, transcendentals=2 * 10**6
        ),
    )(
        xs, gate_in, bc, dt_raw, ids[:, None], ids[None, :], mine, norm_gain[None, :]
    )


def solution(mesh):
    rows = P(("groups", "ctx", "head"), None)
    return jax.shard_map(
        shards,
        mesh=mesh,
        in_specs=(rows, rows, rows, rows, P(("groups", "ctx")), P("head"), P("head"), P("head"), P()),
        out_specs=rows,
        check_vma=False,
    )
```

```python
import functools

import jax
import jax.numpy as jnp
from jax import lax
from jax.experimental import pallas as pl
from jax.experimental.pallas import tpu as pltpu
from jax.sharding import PartitionSpec as P

STATE = 128
EXTRA = 16
WIDTH = 256
LAG = 2
MESH = pl.DeviceIdType.MESH
f32, bf16 = jnp.float32, jnp.bfloat16


def two_parts(v):
    hi = v.astype(bf16)
    return hi, (v - hi.astype(f32)).astype(bf16)


def dot(a, b):
    return jnp.dot(a, b, preferred_element_type=f32)


def kernel(
    n_ctx, n_head, chunks, lag,
    x_hbm, gate_hbm, bc, dt_raw, ids_col, ids_row, mine, backs,
    gated_ref, scale_ref,
    x, gate, into_s, out_s, decay_s, scores_s, last_b, in_c_s, rows_s, par, end_tile, ends, prev,
    state_s, send_r, send_u, send_v, recv_r, recv_u, recv_v, square,
    load_sem, par_ssem, par_rsem, end_ssem, end_rsem, prev_sem, r_ssem, r_rsem, u_ssem, u_rsem, v_ssem, v_rsem,
    weighted,
):
    tokens, columns = x.shape
    heads = dt_raw.shape[1]
    hdim = columns // heads
    own = columns // chunks
    my_ctx, my_head = lax.axis_index("ctx"), lax.axis_index("head")
    has_prev, has_next = my_ctx > 0, my_ctx < n_ctx - 1
    has_low, has_high = my_head > 0, my_head < n_head - 1
    next_ctx = jnp.minimum(my_ctx + 1, n_ctx - 1)
    high = jnp.minimum(my_head + 1, n_head - 1)
    low = jnp.maximum(my_head - 1, 0)

    load_x = pltpu.make_async_copy(x_hbm, x, load_sem.at[0])
    load_gate = pltpu.make_async_copy(gate_hbm, gate, load_sem.at[1])
    load_x.start()
    load_gate.start()

    barrier = pltpu.get_barrier_semaphore()
    for k in range(1, n_head):
        peer = lax.rem(my_head + k, n_head)
        pl.semaphore_signal(barrier, inc=1, device_id={"head": peer}, device_id_type=MESH)

    @pl.when(has_prev)
    def _():
        pl.semaphore_signal(barrier, inc=1, device_id={"ctx": my_ctx - 1}, device_id_type=MESH)

    @pl.when(has_next)
    def _():
        pl.semaphore_signal(barrier, inc=1, device_id={"ctx": my_ctx + 1}, device_id_type=MESH)

    neighbours = jnp.minimum(my_ctx, 1) + jnp.minimum(n_ctx - 1 - my_ctx, 1)
    pl.semaphore_wait(barrier, n_head - 1 + neighbours)

    def tile_copy(src, dst, ssem, rsem, slot, peer, sem):
        return pltpu.make_async_remote_copy(
            src_ref=src, dst_ref=dst.at[slot], send_sem=ssem.at[sem], recv_sem=rsem.at[slot],
            device_id={"head": peer}, device_id_type=MESH,
        )

    prev_copy = pltpu.make_async_remote_copy(
        src_ref=backs, dst_ref=prev, send_sem=prev_sem.at[0], recv_sem=prev_sem.at[1],
        device_id={"ctx": next_ctx}, device_id_type=MESH,
    )
    peers = [lax.rem(my_head + k, n_head) for k in range(1, n_head)]
    for peer in peers:
        tile_copy(mine, par, par_ssem, par_rsem, my_head, peer, peer).start()
    pl.when(has_next)(prev_copy.start)

    in_b, in_c = bc[:, :STATE], bc[:, STATE:]
    scores = lax.dot_general(in_c, in_b, (((1,), (1,)), ((), ())), preferred_element_type=f32)
    lower = lax.broadcasted_iota(jnp.int32, (tokens, tokens), 0) >= lax.broadcasted_iota(
        jnp.int32, (tokens, tokens), 1
    )
    same = ids_col[...] == ids_row[...]
    scores_s[...] = jnp.where(lower & same, scores, 0.0).astype(bf16)
    last_id = ids_row[:, tokens - 1 : tokens]
    last_b[...] = jnp.where(ids_col[...] == last_id, in_b.astype(f32), 0.0).astype(bf16)

    for peer in peers:
        tile_copy(mine, par, par_ssem, par_rsem, peer, peer, peer).wait_recv()
    par[my_head] = mine[...]
    params = par[0]
    for k in range(1, n_head):
        params = params + par[k]
    bias, rate, skip = params[0:1, :heads], params[1:2, :heads], params[2:3, :heads]

    v = dt_raw[...].astype(f32) + bias
    dt = jnp.maximum(v, 0.0) + jnp.log1p(jnp.exp(-jnp.abs(v)))
    step = dt * rate
    step_hi = step.astype(bf16)
    rest, step_lo = two_parts(step - step_hi.astype(f32))
    ones = lower.astype(f32).astype(bf16)
    log_decay = -(dot(ones, step_hi) + dot(ones, rest) + dot(ones, step_lo))
    log_end = log_decay[tokens - 1 : tokens, :]
    end_tile[...] = jnp.zeros_like(end_tile)
    end_tile[0:1, :heads] = log_end
    for peer in peers:
        tile_copy(end_tile, ends, end_ssem, end_rsem, my_head, peer, peer).start()
    middle = 0.5 * log_end
    for ref, value in (
        (into_s, jnp.exp(middle - log_decay) * dt),
        (out_s, jnp.exp(log_decay - middle)),
        (decay_s, jnp.exp(log_decay)),
    ):
        ref[0], ref[1] = two_parts(value)

    @pl.when(my_ctx == 0)
    def _():
        prev[...] = jnp.full(prev.shape, -1.0, f32)
        recv_r[...] = jnp.zeros_like(recv_r)

    @pl.when(my_head == 0)
    def _():
        recv_u[...] = jnp.zeros_like(recv_u)

    @pl.when(my_head == n_head - 1)
    def _():
        recv_v[...] = jnp.zeros_like(recv_v)

    pl.when(has_prev)(prev_copy.wait_recv)
    for peer in peers:
        tile_copy(end_tile, ends, end_ssem, end_rsem, peer, peer, peer).wait_recv()
    ends[my_head] = end_tile[...]
    before = prev[n_head - 1 : n_head, :]
    my_before = before
    one = jnp.ones((1, heads), f32)
    ahead, through, after, whole, mine_m = one, one, one, one, one
    for z in range(n_head):
        back = backs[z : z + 1, :]
        my_before = jnp.where(my_head == z, before, my_before)
        m = jnp.where(back == before, jnp.exp(ends[z, 0:1, :]), 0.0)[:, :heads]
        before = back
        whole = whole * m
        ahead = jnp.where(z < my_head, ahead * m, ahead)
        through = jnp.where(z <= my_head, through * m, through)
        after = jnp.where(z > my_head, after * m, after)
        mine_m = jnp.where(my_head == z, m, mine_m)
    in_c_s[...] = jnp.where(
        ids_col[...].astype(f32) == my_before[:, 0:1], in_c.astype(f32), 0.0
    ).astype(bf16)
    at = lax.broadcasted_iota(jnp.int32, (EXTRA, heads), 0)
    pick = jnp.zeros((EXTRA, heads), f32)
    for i, row in enumerate((jnp.exp(middle), skip, mine_m, ahead, through, after, whole)):
        top = row.astype(bf16).astype(f32)
        pick = jnp.where(at == 2 * i, top, pick)
        pick = jnp.where(at == 2 * i + 1, row - top, pick)
    rows_s[...] = pick.astype(bf16)
    square[...] = jnp.zeros_like(square)
    load_x.wait()
    load_gate.wait()

    def selector(g):
        head = lax.broadcasted_iota(jnp.int32, (heads, own), 0)
        column = lax.broadcasted_iota(jnp.int32, (heads, own), 1) + g * own
        base = head * hdim
        return jnp.where((column >= base) & (column < base + hdim), 1.0, 0.0).astype(bf16)

    def spread(ref, sel):
        return dot(ref[0], sel) + dot(ref[1], sel)

    def part(g):
        return pl.ds(pl.multiple_of(g * own, own), own)

    def spread_rows(sel):
        extra = dot(rows_s[...], sel)
        return [extra[2 * i : 2 * i + 1] + extra[2 * i + 1 : 2 * i + 2] for i in range(7)]

    def chain(src, dst, ssem, rsem, g, to):
        return pltpu.make_async_remote_copy(
            src_ref=src.at[g], dst_ref=dst.at[g], send_sem=ssem.at[g], recv_sem=rsem.at[g],
            device_id=to, device_id_type=MESH,
        )

    def copy_r(g):
        return chain(send_r, recv_r, r_ssem, r_rsem, g, {"ctx": next_ctx})

    def copy_u(g):
        return chain(send_u, recv_u, u_ssem, u_rsem, g, {"head": high})

    def copy_v(g):
        return chain(send_v, recv_v, v_ssem, v_rsem, g, {"head": low})

    def first(g):
        sel = selector(g)
        mid, _, _, _, _, after_g, whole_g = spread_rows(sel)
        w = (spread(into_s, sel) * x[:, part(g)].astype(f32)).astype(bf16)
        weighted[:, part(g)] = w
        state = mid * lax.dot_general(
            last_b[...], w, (((0,), (0,)), ((), ())), preferred_element_type=f32
        )
        state_s[g] = state

        @pl.when(has_prev)
        def _():
            copy_r(g).wait_recv()

        @pl.when(has_next)
        def _():
            send_r[g] = (whole_g * recv_r[g].astype(f32) + after_g * state).astype(bf16)
            copy_r(g).start()

    def upward(g):
        @pl.when(has_low)
        def _():
            copy_u(g).wait_recv()

        @pl.when(has_high)
        def _():
            _, _, m, _, through_g, _, _ = spread_rows(selector(g))
            send_u[g] = (
                m * recv_u[g].astype(f32) + state_s[g] + through_g * recv_r[g].astype(f32)
            ).astype(bf16)
            copy_u(g).start()

    def downward(g):
        @pl.when(has_high)
        def _():
            copy_v(g).wait_recv()

        @pl.when(has_low)
        def _():
            send_v[g] = (recv_v[g].astype(f32) + recv_r[g].astype(f32)).astype(bf16)
            copy_v(g).start()

    def finish(g):
        sel = selector(g)
        cols = part(g)
        mid, skips, _, ahead_g, _, _, _ = spread_rows(sel)
        entering = recv_u[g].astype(f32) + ahead_g * (
            recv_v[g].astype(f32) + recv_r[g].astype(f32)
        )
        y = dot(scores_s[...], weighted[:, cols])
        carried = dot(in_c_s[...], entering.astype(bf16))
        ssm = (
            spread(out_s, sel) * y
            + spread(decay_s, sel) * carried
            + skips * x[:, cols].astype(f32)
        )
        v = gate[:, cols].astype(f32)
        gated = ssm.astype(bf16).astype(f32) * (v / (1.0 + jnp.exp(-v)))
        gated_ref[:, cols] = gated.astype(bf16)
        total = square[...]
        for i in range(own // 128):
            piece = gated[:, i * 128 : (i + 1) * 128]
            total = total + piece * piece
        square[...] = total

    up_lag = lag * my_head
    down_lag = lag * (n_head - 1 - my_head)
    end_lag = lag * (n_head - 1)

    def turn(i, carry):
        for stage, behind in ((first, 0), (upward, up_lag), (downward, down_lag), (finish, end_lag)):
            g = i - behind

            @pl.when((g >= 0) & (g < chunks))
            def _(stage=stage, g=g):
                stage(g)

        return carry

    lax.fori_loop(0, chunks + end_lag, turn, 0)
    mean = jnp.sum(square[...], axis=1, keepdims=True) * (1.0 / columns)
    scale_ref[...] = jnp.broadcast_to(lax.rsqrt(mean + 1e-05), scale_ref.shape)

    for peer in peers:
        tile_copy(mine, par, par_ssem, par_rsem, my_head, peer, peer).wait_send()
        tile_copy(end_tile, ends, end_ssem, end_rsem, my_head, peer, peer).wait_send()
    pl.when(has_next)(prev_copy.wait_send)

    def drain(g, carry):
        pl.when(has_next)(copy_r(g).wait_send)
        pl.when(has_high)(copy_u(g).wait_send)
        pl.when(has_low)(copy_v(g).wait_send)
        return carry

    lax.fori_loop(0, chunks, drain, 0)


def shards(xs, gate_in, bc, dt_raw, doc_ids, dt_bias, decay_rate, skip, norm_gain):
    tokens, columns = xs.shape
    heads = dt_raw.shape[1]
    n_ctx, n_head = lax.axis_size("ctx"), lax.axis_size("head")
    chunks = columns // WIDTH
    at = lax.axis_index("head")
    ids = lax.dynamic_slice(doc_ids, (at * tokens,), (tokens,))
    stack = jnp.stack([dt_bias, decay_rate, skip])
    mine = jnp.where(
        (jnp.arange(heads) // (heads // n_head) == at)[None, :], jnp.tile(stack, (1, n_head)), 0.0
    )
    mine = jnp.pad(mine, ((0, 5), (0, 128 - heads)))
    tall = max(8, n_head)
    backs = doc_ids.reshape(n_head, tokens)[:, -1].astype(f32)
    backs = jnp.broadcast_to(jnp.pad(backs, (0, tall - n_head))[:, None], (tall, 128))
    vmem = pl.BlockSpec(memory_space=pltpu.VMEM)
    hbm = pl.BlockSpec(memory_space=pl.ANY)
    dma = pltpu.SemaphoreType.DMA
    travel = pltpu.VMEM((chunks, STATE, WIDTH), bf16)
    pair = pltpu.VMEM((2, tokens, heads), bf16)
    gated, scale = pl.pallas_call(
        functools.partial(kernel, n_ctx, n_head, chunks, LAG),
        out_shape=(
            jax.ShapeDtypeStruct((tokens, columns), bf16),
            jax.ShapeDtypeStruct((tokens, 128), f32),
        ),
        in_specs=[hbm, hbm] + [vmem] * 6,
        out_specs=(vmem, vmem),
        scratch_shapes=[
            pltpu.VMEM((tokens, columns), bf16),
            pltpu.VMEM((tokens, columns), bf16),
            pair, pair, pair,
            pltpu.VMEM((tokens, tokens), bf16),
            pltpu.VMEM((tokens, STATE), bf16),
            pltpu.VMEM((tokens, STATE), bf16),
            pltpu.VMEM((EXTRA, heads), bf16),
            pltpu.VMEM((n_head, 8, 128), f32),
            pltpu.VMEM((8, 128), f32),
            pltpu.VMEM((n_head, 8, 128), f32),
            pltpu.VMEM((tall, 128), f32),
            pltpu.VMEM((chunks, STATE, WIDTH), f32),
            travel, travel, travel, travel, travel, travel,
            pltpu.VMEM((tokens, 128), f32),
            dma((2,)), dma((n_head,)), dma((n_head,)), dma((n_head,)), dma((n_head,)), dma((2,)),
        ]
        + [dma((chunks,))] * 6
        + [pltpu.VMEM((tokens, columns), bf16)],
        compiler_params=pltpu.CompilerParams(
            collective_id=0, has_side_effects=True, vmem_limit_bytes=44 * 2**20
        ),
        cost_estimate=pl.CostEstimate(
            flops=3 * 10**9, bytes_accessed=10**7, transcendentals=2 * 10**6
        ),
    )(xs, gate_in, bc, dt_raw, ids[:, None], ids[None, :], mine, backs)
    return (gated.astype(f32) * scale[:, :1] * norm_gain[None, :]).astype(bf16)


def solution(mesh):
    rows = P(("groups", "ctx", "head"), None)
    return jax.shard_map(
        shards,
        mesh=mesh,
        in_specs=(rows, rows, rows, rows, P(("groups", "ctx")), P("head"), P("head"), P("head"), P()),
        out_specs=rows,
        check_vma=False,
    )
```

```python
import functools

import jax
import jax.numpy as jnp
from jax import lax
from jax.experimental import pallas as pl
from jax.experimental.pallas import tpu as pltpu
from jax.sharding import PartitionSpec as P

STATE = 128
EXTRA = 16
WIDTH = 256
LAG = 3
MESH = pl.DeviceIdType.MESH
f32, bf16 = jnp.float32, jnp.bfloat16


def two_parts(v):
    hi = v.astype(bf16)
    return hi, (v - hi.astype(f32)).astype(bf16)


def dot(a, b):
    return jnp.dot(a, b, preferred_element_type=f32)


def kernel(
    n_ctx, n_head, chunks, lag,
    x_hbm, gate_hbm, bc, dt_raw, ids_col, ids_row, mine, backs,
    gated_ref, scale_ref,
    x, gate, into_s, out_s, decay_s, scores_s, last_b, in_c_s, rows_s, par, end_tile, ends, prev,
    state_s, send_r, send_u, send_v, recv_r, recv_u, recv_v, square,
    load_sem, par_ssem, par_rsem, end_ssem, end_rsem, prev_sem, r_ssem, r_rsem, u_ssem, u_rsem, v_ssem, v_rsem,
    weighted, sels,
):
    tokens, columns = x.shape
    heads = dt_raw.shape[1]
    hdim = columns // heads
    own = columns // chunks
    my_ctx, my_head = lax.axis_index("ctx"), lax.axis_index("head")
    has_prev, has_next = my_ctx > 0, my_ctx < n_ctx - 1
    has_low, has_high = my_head > 0, my_head < n_head - 1
    next_ctx = jnp.minimum(my_ctx + 1, n_ctx - 1)
    high = jnp.minimum(my_head + 1, n_head - 1)
    low = jnp.maximum(my_head - 1, 0)

    load_x = pltpu.make_async_copy(x_hbm, x, load_sem.at[0])
    load_gate = pltpu.make_async_copy(gate_hbm, gate, load_sem.at[1])
    load_x.start()
    load_gate.start()

    barrier = pltpu.get_barrier_semaphore()
    for k in range(1, n_head):
        peer = lax.rem(my_head + k, n_head)
        pl.semaphore_signal(barrier, inc=1, device_id={"head": peer}, device_id_type=MESH)

    @pl.when(has_prev)
    def _():
        pl.semaphore_signal(barrier, inc=1, device_id={"ctx": my_ctx - 1}, device_id_type=MESH)

    @pl.when(has_next)
    def _():
        pl.semaphore_signal(barrier, inc=1, device_id={"ctx": my_ctx + 1}, device_id_type=MESH)

    def make_selector(g, carry):
        row = lax.broadcasted_iota(jnp.int32, (2 * heads, own), 0)
        base = jnp.where(row >= heads, row - heads, row) * hdim
        column = lax.broadcasted_iota(jnp.int32, (2 * heads, own), 1) + g * own
        sels[g] = jnp.where((column >= base) & (column < base + hdim), 1.0, 0.0).astype(bf16)
        return carry

    lax.fori_loop(0, chunks, make_selector, 0)
    neighbours = jnp.minimum(my_ctx, 1) + jnp.minimum(n_ctx - 1 - my_ctx, 1)
    pl.semaphore_wait(barrier, n_head - 1 + neighbours)

    def tile_copy(src, dst, ssem, rsem, slot, peer, sem):
        return pltpu.make_async_remote_copy(
            src_ref=src, dst_ref=dst.at[slot], send_sem=ssem.at[sem], recv_sem=rsem.at[slot],
            device_id={"head": peer}, device_id_type=MESH,
        )

    prev_copy = pltpu.make_async_remote_copy(
        src_ref=backs, dst_ref=prev, send_sem=prev_sem.at[0], recv_sem=prev_sem.at[1],
        device_id={"ctx": next_ctx}, device_id_type=MESH,
    )
    peers = [lax.rem(my_head + k, n_head) for k in range(1, n_head)]
    for peer in peers:
        tile_copy(mine, par, par_ssem, par_rsem, my_head, peer, peer).start()
    pl.when(has_next)(prev_copy.start)

    in_b, in_c = bc[:, :STATE], bc[:, STATE:]
    scores = lax.dot_general(in_c, in_b, (((1,), (1,)), ((), ())), preferred_element_type=f32)
    lower = lax.broadcasted_iota(jnp.int32, (tokens, tokens), 0) >= lax.broadcasted_iota(
        jnp.int32, (tokens, tokens), 1
    )
    same = ids_col[...] == ids_row[...]
    scores_s[...] = jnp.where(lower & same, scores, 0.0).astype(bf16)
    last_id = ids_row[:, tokens - 1 : tokens]
    last_b[...] = jnp.where(ids_col[...] == last_id, in_b.astype(f32), 0.0).T.astype(bf16)

    for peer in peers:
        tile_copy(mine, par, par_ssem, par_rsem, peer, peer, peer).wait_recv()
    par[my_head] = mine[...]
    params = par[0]
    for k in range(1, n_head):
        params = params + par[k]
    bias, rate, skip = params[0:1, :heads], params[1:2, :heads], params[2:3, :heads]

    v = dt_raw[...].astype(f32) + bias
    dt = jnp.maximum(v, 0.0) + jnp.log1p(jnp.exp(-jnp.abs(v)))
    step = dt * rate
    step_hi = step.astype(bf16)
    rest, step_lo = two_parts(step - step_hi.astype(f32))
    ones = lower.astype(f32).astype(bf16)
    log_decay = -(dot(ones, step_hi) + dot(ones, rest) + dot(ones, step_lo))
    log_end = log_decay[tokens - 1 : tokens, :]
    end_tile[...] = jnp.zeros_like(end_tile)
    end_tile[0:1, :heads] = log_end
    for peer in peers:
        tile_copy(end_tile, ends, end_ssem, end_rsem, my_head, peer, peer).start()
    middle = 0.5 * log_end
    for ref, value in (
        (into_s, jnp.exp(middle - log_decay) * dt),
        (out_s, jnp.exp(log_decay - middle)),
        (decay_s, jnp.exp(log_decay)),
    ):
        ref[:, :heads], ref[:, heads:] = two_parts(value)

    @pl.when(my_ctx == 0)
    def _():
        prev[...] = jnp.full(prev.shape, -1.0, f32)
        recv_r[...] = jnp.zeros_like(recv_r)

    @pl.when(my_head == 0)
    def _():
        recv_u[...] = jnp.zeros_like(recv_u)

    @pl.when(my_head == n_head - 1)
    def _():
        recv_v[...] = jnp.zeros_like(recv_v)

    pl.when(has_prev)(prev_copy.wait_recv)
    for peer in peers:
        tile_copy(end_tile, ends, end_ssem, end_rsem, peer, peer, peer).wait_recv()
    ends[my_head] = end_tile[...]
    before = prev[n_head - 1 : n_head, :]
    my_before = before
    one = jnp.ones((1, heads), f32)
    ahead, through, after, whole, mine_m = one, one, one, one, one
    for z in range(n_head):
        back = backs[z : z + 1, :]
        my_before = jnp.where(my_head == z, before, my_before)
        m = jnp.where(back == before, jnp.exp(ends[z, 0:1, :]), 0.0)[:, :heads]
        before = back
        whole = whole * m
        ahead = jnp.where(z < my_head, ahead * m, ahead)
        through = jnp.where(z <= my_head, through * m, through)
        after = jnp.where(z > my_head, after * m, after)
        mine_m = jnp.where(my_head == z, m, mine_m)
    in_c_s[...] = jnp.where(
        ids_col[...].astype(f32) == my_before[:, 0:1], in_c.astype(f32), 0.0
    ).astype(bf16)
    at = lax.broadcasted_iota(jnp.int32, (EXTRA, heads), 0)
    pick = jnp.zeros((EXTRA, heads), f32)
    for i, row in enumerate((jnp.exp(middle), skip, mine_m, ahead, through, after, whole)):
        top = row.astype(bf16).astype(f32)
        pick = jnp.where(at == 2 * i, top, pick)
        pick = jnp.where(at == 2 * i + 1, row - top, pick)
    rows_s[...] = pick.astype(bf16)
    square[...] = jnp.zeros_like(square)
    load_x.wait()
    load_gate.wait()

    def selector(g):
        return sels[g]

    def spread(ref, sel):
        return dot(ref[...], sel)

    def part(g):
        return pl.ds(pl.multiple_of(g * own, own), own)

    def spread_rows(sel):
        extra = dot(rows_s[...], sel[:heads])
        return [extra[2 * i : 2 * i + 1] + extra[2 * i + 1 : 2 * i + 2] for i in range(7)]

    def chain(src, dst, ssem, rsem, g, to):
        return pltpu.make_async_remote_copy(
            src_ref=src.at[g], dst_ref=dst.at[g], send_sem=ssem.at[g], recv_sem=rsem.at[g],
            device_id=to, device_id_type=MESH,
        )

    def copy_r(g):
        return chain(send_r, recv_r, r_ssem, r_rsem, g, {"ctx": next_ctx})

    def copy_u(g):
        return chain(send_u, recv_u, u_ssem, u_rsem, g, {"head": high})

    def copy_v(g):
        return chain(send_v, recv_v, v_ssem, v_rsem, g, {"head": low})

    def first(g):
        sel = selector(g)
        mid, _, _, _, _, after_g, whole_g = spread_rows(sel)
        w = (spread(into_s, sel) * x[:, part(g)].astype(f32)).astype(bf16)
        weighted[:, part(g)] = w
        state = mid * dot(last_b[...], w)
        state_s[g] = state

        @pl.when(has_prev)
        def _():
            copy_r(g).wait_recv()

        @pl.when(has_next)
        def _():
            send_r[g] = (whole_g * recv_r[g].astype(f32) + after_g * state).astype(bf16)
            copy_r(g).start()

    def upward(g):
        @pl.when(has_low)
        def _():
            copy_u(g).wait_recv()

        @pl.when(has_high)
        def _():
            _, _, m, _, through_g, _, _ = spread_rows(selector(g))
            send_u[g] = (
                m * recv_u[g].astype(f32) + state_s[g] + through_g * recv_r[g].astype(f32)
            ).astype(bf16)
            copy_u(g).start()

    def downward(g):
        @pl.when(has_high)
        def _():
            copy_v(g).wait_recv()

        @pl.when(has_low)
        def _():
            send_v[g] = (recv_v[g].astype(f32) + recv_r[g].astype(f32)).astype(bf16)
            copy_v(g).start()

    def finish(g):
        sel = selector(g)
        cols = part(g)
        mid, skips, _, ahead_g, _, _, _ = spread_rows(sel)
        entering = recv_u[g].astype(f32) + ahead_g * (
            recv_v[g].astype(f32) + recv_r[g].astype(f32)
        )
        y = dot(scores_s[...], weighted[:, cols])
        carried = dot(in_c_s[...], entering.astype(bf16))
        ssm = (
            spread(out_s, sel) * y
            + spread(decay_s, sel) * carried
            + skips * x[:, cols].astype(f32)
        )
        v = gate[:, cols].astype(f32)
        gated = ssm.astype(bf16).astype(f32) * (v / (1.0 + jnp.exp(-v)))
        gated_ref[:, cols] = gated.astype(bf16)
        total = square[...]
        for i in range(own // 128):
            piece = gated[:, i * 128 : (i + 1) * 128]
            total = total + piece * piece
        square[...] = total

    up_lag = lag * my_head
    down_lag = lag * (n_head - 1 - my_head)
    end_lag = lag * (n_head - 1)

    def turn(i, carry):
        for stage, behind in ((first, 0), (upward, up_lag), (downward, down_lag), (finish, end_lag)):
            g = i - behind

            @pl.when((g >= 0) & (g < chunks))
            def _(stage=stage, g=g):
                stage(g)

        return carry

    lax.fori_loop(0, chunks + end_lag, turn, 0)
    mean = jnp.sum(square[...], axis=1, keepdims=True) * (1.0 / columns)
    scale_ref[...] = jnp.broadcast_to(lax.rsqrt(mean + 1e-05), scale_ref.shape)

    for peer in peers:
        tile_copy(mine, par, par_ssem, par_rsem, my_head, peer, peer).wait_send()
        tile_copy(end_tile, ends, end_ssem, end_rsem, my_head, peer, peer).wait_send()
    pl.when(has_next)(prev_copy.wait_send)

    def drain(g, carry):
        pl.when(has_next)(copy_r(g).wait_send)
        pl.when(has_high)(copy_u(g).wait_send)
        pl.when(has_low)(copy_v(g).wait_send)
        return carry

    lax.fori_loop(0, chunks, drain, 0)


def shards(xs, gate_in, bc, dt_raw, doc_ids, dt_bias, decay_rate, skip, norm_gain):
    tokens, columns = xs.shape
    heads = dt_raw.shape[1]
    n_ctx, n_head = lax.axis_size("ctx"), lax.axis_size("head")
    chunks = columns // WIDTH
    at = lax.axis_index("head")
    ids = lax.dynamic_slice(doc_ids, (at * tokens,), (tokens,))
    stack = jnp.stack([dt_bias, decay_rate, skip])
    mine = jnp.where(
        (jnp.arange(heads) // (heads // n_head) == at)[None, :], jnp.tile(stack, (1, n_head)), 0.0
    )
    mine = jnp.pad(mine, ((0, 5), (0, 128 - heads)))
    tall = max(8, n_head)
    backs = doc_ids.reshape(n_head, tokens)[:, -1].astype(f32)
    backs = jnp.broadcast_to(jnp.pad(backs, (0, tall - n_head))[:, None], (tall, 128))
    vmem = pl.BlockSpec(memory_space=pltpu.VMEM)
    hbm = pl.BlockSpec(memory_space=pltpu.HBM)
    dma = pltpu.SemaphoreType.DMA
    travel = pltpu.VMEM((chunks, STATE, WIDTH), bf16)
    pair = pltpu.VMEM((tokens, 2 * heads), bf16)
    gated, scale = pl.pallas_call(
        functools.partial(kernel, n_ctx, n_head, chunks, LAG),
        out_shape=(
            jax.ShapeDtypeStruct((tokens, columns), bf16),
            jax.ShapeDtypeStruct((tokens, 128), f32),
        ),
        in_specs=[hbm, hbm] + [vmem] * 6,
        out_specs=(vmem, vmem),
        scratch_shapes=[
            pltpu.VMEM((tokens, columns), bf16),
            pltpu.VMEM((tokens, columns), bf16),
            pair, pair, pair,
            pltpu.VMEM((tokens, tokens), bf16),
            pltpu.VMEM((STATE, tokens), bf16),
            pltpu.VMEM((tokens, STATE), bf16),
            pltpu.VMEM((EXTRA, heads), bf16),
            pltpu.VMEM((n_head, 8, 128), f32),
            pltpu.VMEM((8, 128), f32),
            pltpu.VMEM((n_head, 8, 128), f32),
            pltpu.VMEM((tall, 128), f32),
            pltpu.VMEM((chunks, STATE, WIDTH), f32),
            travel, travel, travel, travel, travel, travel,
            pltpu.VMEM((tokens, 128), f32),
            dma((2,)), dma((n_head,)), dma((n_head,)), dma((n_head,)), dma((n_head,)), dma((2,)),
        ]
        + [dma((chunks,))] * 6
        + [
            pltpu.VMEM((tokens, columns), bf16),
            pltpu.VMEM((chunks, 2 * heads, WIDTH), bf16),
        ],
        compiler_params=pltpu.CompilerParams(
            collective_id=0, has_side_effects=True, vmem_limit_bytes=49 * 2**20
        ),
        cost_estimate=pl.CostEstimate(
            flops=3 * 10**9, bytes_accessed=10**7, transcendentals=2 * 10**6
        ),
    )(xs, gate_in, bc, dt_raw, ids[:, None], ids[None, :], mine, backs)
    return (gated.astype(f32) * scale[:, :1] * norm_gain[None, :]).astype(bf16)


def solution(mesh):
    rows = P(("groups", "ctx", "head"), None)
    return jax.shard_map(
        shards,
        mesh=mesh,
        in_specs=(rows, rows, rows, rows, P(("groups", "ctx")), P("head"), P("head"), P("head"), P()),
        out_specs=rows,
        check_vma=False,
    )
```
